32 devices in a mesh: parts: 2 (over x), dp: 16 (over z, y, core).
Axes of the slice: x: 2, y: 2, z: 4, core: 2. Of those that a mesh axis runs over, the one named last changes fastest.
Arguments:
- mixer_in: bfloat16 [8192, 8192], P(('parts', 'dp')), parts along dimension 0, may hold values from -6 to 6
- gate_in: bfloat16 [8192, 8192], P(('parts', 'dp')), parts along dimension 0, may hold values from -8 to 8
- conv_weight: bfloat16 [4, 8192], replicated, may hold values from -3 to 3
- conv_bias: bfloat16 [8192], replicated, may hold values from -3 to 3
- x_weight: bfloat16 [8192, 288], P('dp'), may hold values from -0.09375 to 0.09375
- dt_weight: bfloat16 [256, 8192], P(None, 'dp'), may hold values from -0.375 to 0.375
- dt_bias: bfloat16 [8192], P('dp'), may hold values from -7 to -2
- a_log: float32 [16, 8192], P(None, 'dp'), may hold values from -3 to 1.5
- d_skip: float32 [8192], P('dp'), may hold values from -4 to 4
- block_slot: int32 [64], P('parts'), parts along dimension 0, may hold values from 0 to 39, as said below
- block_first: int32 [64], P('parts'), parts along dimension 0, may hold values from 0 to 1, as said below
- block_live: int32 [64], P('parts'), parts along dimension 0, may hold values from 1 to 128, as said below
Outputs:
- gated: bfloat16 [8192, 8192], P(('parts', 'dp')), parts along dimension 0
The draws below stay inside these ranges and needn't reach their ends.
There are 2 independent parts, one for each index of `parts`. The reference program is written for one: setup_inputs(seed, part) draws one part's arguments, and reference() takes and returns one part's arrays. A program takes and returns all parts, laid end to end along the dimension named above; an argument that names none is the same for every part. Nothing has to cross between parts.
Inputs may be any that keep to these rules, and one draw needn't show every extreme that they name: `block_slot`: the values are distinct slots. The blocks of one row are consecutive in the incoming order and fill consecutive slots of one lane in that order; a lane holds whole rows; the last lane has all 10 slots used; slot 0 is used; the first block in the incoming order begins a row. `block_first`: agrees with block_slot: 1 exactly for the first block of each row. `block_live`: only the last block of a row can hold fewer than 128 live tokens.
All inputs are finite; a program needn't handle non-finite values.
Results may differ from the reference program's by a relative error of at most 0.0086.
Values may be sent and summed in bfloat16 or wider, within the bound.
A program may use at most 128 MiB of HBM per device.

```python
import jax
import jax.numpy as jnp
from jax import lax

INNER = 8192
STATE = 16
KERNEL = 4
DT_RANK = 256
BLK = 128
TOKENS = 4096
BLOCKS = 32
LANES = 4
LANE_LEN = 10


def lane_layout(key):
    slots = LANES * LANE_LEN
    excess = slots - BLOCKS
    key_pick = jax.random.fold_in(key, 1)
    key_start = jax.random.fold_in(key, 2)
    key_order = jax.random.fold_in(key, 3)
    key_live = jax.random.fold_in(key, 4)
    index = jnp.arange(slots, dtype=jnp.int32)
    lane_of = index // LANE_LEN
    place = index % LANE_LEN
    full_lane = LANES - 1
    priority = jax.random.permutation(key_pick, slots).astype(jnp.int32)
    priority = jnp.where((lane_of == full_lane) | (index == 0), slots + priority, priority)
    rank = jnp.argsort(jnp.argsort(priority))
    picked = (rank < excess).astype(jnp.int32)
    lane_ids = jnp.arange(LANES, dtype=jnp.int32)
    removed = jnp.sum(picked[None, :] * (lane_of[None, :] == lane_ids[:, None]).astype(jnp.int32), axis=1)
    keep = LANE_LEN - removed
    used = place < keep[lane_of]
    coin = jax.random.randint(key_start, (slots,), 0, 3)
    starts = (place == 0) | (coin == 0) & (place != 1)
    start_index = lax.cummax(jnp.where(starts, index, 0), axis=0)
    row_key = jax.random.permutation(key_order, slots).astype(jnp.int32)[start_index]
    sort_key = jnp.where(used, row_key * slots + (index - start_index), slots * slots + index)
    order = jnp.argsort(sort_key)[:BLOCKS].astype(jnp.int32)
    next_start = jnp.concatenate([starts[1:] | ~used[1:], jnp.ones((1,), bool)], 0)
    is_last = next_start | (place == LANE_LEN - 1)
    live_draw = jax.random.randint(key_live, (slots,), 1, BLK + 1)
    live = jnp.where(is_last, live_draw, BLK).astype(jnp.int32)
    return (order, starts[order].astype(jnp.int32), live[order])


def draw_block_slot(key, part):
    return lane_layout(key)[0]


def draw_block_first(key, part):
    return lane_layout(key)[1]


def draw_block_live(key, part):
    return lane_layout(key)[2]


def level_of(key, shape, pieces, smallest, high):
    def one(position, shards_of):
        draws = jax.random.uniform(jax.random.fold_in(jax.random.fold_in(key, 6), position), (shards_of,), jnp.float32, smallest / len(pieces), high / len(pieces))
        return jnp.repeat(jnp.exp(draws), shape[position] // shards_of).reshape((-1,) + (1,) * (len(shape) - position - 1))

    gain = one(*pieces[0])
    for cut in pieces[1:]:
        gain = gain * one(*cut)
    return gain


def bell_draw(rng, dims, deviation, limit, shards=(), kind=jnp.bfloat16):
    values = deviation * jax.random.normal(rng, dims, jnp.float32)
    if shards:
        values = values * level_of(rng, dims, shards, -0.22, 0.18)
    return jnp.clip(values, -limit, limit).astype(kind)


def setup_inputs(seed: int = 0, part: int = 0) -> dict:
    splits = jax.random.split(jax.random.key(seed), 13)
    part_splits = jax.random.split(jax.random.fold_in(splits[12], part), 13)
    mixer_in = bell_draw(part_splits[0], (TOKENS, INNER), 1.0, 6.0, ((0, 16),))
    gate_in = bell_draw(part_splits[1], (TOKENS, INNER), 1.5, 8.0, ((0, 16),))
    conv_weight = bell_draw(splits[2], (KERNEL, INNER), KERNEL ** -0.5, 3.0)
    conv_bias = bell_draw(splits[3], (INNER,), 0.5, 3.0)
    x_weight = bell_draw(splits[4], (INNER, DT_RANK + 2 * STATE), (INNER // 2) ** -0.5, 0.09375, ((0, 16),))
    dt_weight = bell_draw(splits[5], (DT_RANK, INNER), DT_RANK ** -0.5, 0.375, ((1, 16),))
    dt_bias = jnp.clip(-7.0 + 5.0 * jax.random.uniform(splits[6], (INNER,), jnp.float32) ** level_of(splits[6], (INNER,), ((0, 16),), -0.2, 0.2), -7.0, -2.0).astype(jnp.bfloat16)
    a_log = jnp.clip(-3.0 + 4.5 * jax.random.uniform(splits[7], (STATE, INNER), jnp.float32) ** level_of(splits[7], (STATE, INNER), ((1, 16),), -0.2, 0.2), -3.0, 1.5)
    d_skip = bell_draw(splits[8], (INNER,), 1.0, 4.0, ((0, 16),), jnp.float32)
    block_slot = draw_block_slot(jax.random.fold_in(jax.random.fold_in(splits[12], part), 71), part)
    block_first = draw_block_first(jax.random.fold_in(jax.random.fold_in(splits[12], part), 71), part)
    block_live = draw_block_live(jax.random.fold_in(jax.random.fold_in(splits[12], part), 71), part)
    return {"mixer_in": mixer_in, "gate_in": gate_in, "conv_weight": conv_weight, "conv_bias": conv_bias, "x_weight": x_weight, "dt_weight": dt_weight, "dt_bias": dt_bias, "a_log": a_log, "d_skip": d_skip, "block_slot": block_slot, "block_first": block_first, "block_live": block_live}


def conv_part(padded, conv_weight, conv_bias, first_tok, offset):
    count = first_tok.shape[0]
    acc = jnp.zeros((count, conv_weight.shape[1]), jnp.float32) + conv_bias.astype(jnp.float32)[None]
    for tap in range(KERNEL):
        back = KERNEL - 1 - tap
        valid = (first_tok == 0) | (offset >= back)
        term = padded[tap:tap + count].astype(jnp.float32) * conv_weight[tap].astype(jnp.float32)[None]
        acc = acc + jnp.where(valid[:, None], term, 0.0)
    return jax.nn.silu(acc).astype(jnp.bfloat16)


def scan_step(rate, skip, carry, inputs):
    conv_now, delta_now, maps_now, start_now = inputs
    width = rate.shape[0]
    step = delta_now.astype(jnp.float32)
    signal = conv_now.astype(jnp.float32)
    in_map = maps_now[:, :width].astype(jnp.float32)
    out_map = maps_now[:, width:].astype(jnp.float32)
    carry = jnp.exp(step[:, None, :] * rate[None]) * (carry * (1.0 - start_now)[:, None, None]) + (step * signal)[:, None, :] * in_map[:, :, None]
    result = jnp.sum(carry * out_map[:, :, None], axis=1) + skip[None] * signal
    return carry, result.astype(jnp.bfloat16)


def reference(mixer_in, gate_in, conv_weight, conv_bias, x_weight, dt_weight, dt_bias, a_log, d_skip, block_slot, block_first, block_live):
    offset = jnp.arange(TOKENS, dtype=jnp.int32) % BLK
    first_tok = jnp.repeat(block_first, BLK)
    padded = jnp.concatenate([jnp.zeros((KERNEL - 1, INNER), jnp.bfloat16), mixer_in], 0)
    convolved = conv_part(padded, conv_weight, conv_bias, first_tok, offset)
    proj = jnp.dot(convolved, x_weight, preferred_element_type=jnp.float32).astype(jnp.bfloat16)
    step_rank = proj[:, :DT_RANK]
    maps = proj[:, DT_RANK:]
    delta = jax.nn.softplus(jnp.dot(step_rank, dt_weight, preferred_element_type=jnp.float32) + dt_bias.astype(jnp.float32)[None]).astype(jnp.bfloat16)
    slots = LANES * LANE_LEN
    positions = LANE_LEN * BLK
    src_of_slot = jnp.full((slots,), BLOCKS, jnp.int32).at[block_slot].set(jnp.arange(BLOCKS, dtype=jnp.int32))

    def to_grid(values):
        cols = values.shape[1]
        blocks = values.reshape(BLOCKS, BLK, cols)
        blocks = jnp.concatenate([blocks, jnp.zeros((1, BLK, cols), values.dtype)], 0)
        grid = blocks[src_of_slot].reshape(LANES, positions, cols)
        return jnp.swapaxes(grid, 0, 1)

    first_slot = jnp.concatenate([block_first, jnp.zeros((1,), jnp.int32)], 0)[src_of_slot]
    at_front = (jnp.arange(BLK, dtype=jnp.int32) == 0).astype(jnp.int32)
    start = (first_slot[:, None] * at_front[None]).reshape(LANES, positions).astype(jnp.float32)
    start = jnp.swapaxes(start, 0, 1)
    rate = -jnp.exp(a_log)
    initial = jnp.zeros((LANES, STATE, INNER), jnp.float32)
    carry, outputs = lax.scan(partial_step(rate, d_skip), initial, (to_grid(convolved), to_grid(delta), to_grid(maps), start))
    outputs = jnp.swapaxes(outputs, 0, 1).reshape(slots, BLK, INNER)
    scanned = outputs[block_slot].reshape(TOKENS, INNER)
    live = offset < jnp.repeat(block_live, BLK)
    gated = scanned.astype(jnp.float32) * jax.nn.silu(gate_in.astype(jnp.float32))
    return jnp.where(live[:, None], gated, 0.0).astype(jnp.bfloat16)


def partial_step(rate, skip):
    def inner(carry, inputs):
        return scan_step(rate, skip, carry, inputs)
    return inner
```

```python
import jax
import jax.numpy as jnp
from jax import lax
from jax.experimental import pallas as pl
from jax.experimental.pallas import tpu as pltpu
from jax.sharding import PartitionSpec as P

BLK = 128
SUB = 8
LANE = 128
HALO = 8
LOG2E = 1.4426950408889634
VMEM_LIMIT = 48 * 1024 * 1024


def passed_along(block, axis, distance):
    devices = range(lax.axis_size(axis))
    route = [(i - distance, i) for i in devices if i - distance in devices]
    return lax.ppermute(block, axis, route)


def params():
    return pltpu.CompilerParams(vmem_limit_bytes=VMEM_LIMIT)


def conv_kernel(first_ref, x_ref, halo_ref, w_ref, b_ref, out_ref):
    taps = w_ref.shape[0]
    w = w_ref[...].astype(jnp.float32)
    bias = b_ref[...].astype(jnp.float32)
    chans = x_ref.shape[1]
    row = lax.broadcasted_iota(jnp.int32, (SUB, chans), 0)
    before = halo_ref[...].astype(jnp.float32)
    for blk in range(x_ref.shape[0] // BLK):
        now = x_ref[blk * BLK : (blk + 1) * BLK, :].astype(jnp.float32)
        before = jnp.where(first_ref[blk] == 0, before, 0.0)
        acc = now * w[taps - 1 : taps] + bias
        for back in range(1, taps):
            rolled = pltpu.roll(now, back, 0)
            head = jnp.where(row < back, pltpu.roll(before, back, 0), rolled[:SUB])
            shifted = jnp.concatenate([head, rolled[SUB:]], 0)
            acc = acc + shifted * w[taps - 1 - back : taps - back]
        out_ref[0, blk * BLK : (blk + 1) * BLK, :] = jax.nn.silu(acc).astype(jnp.bfloat16)
        before = now[BLK - SUB :]


def proj_kernel(conv_ref, w_ref, out_ref, acc_ref):
    step = pl.program_id(0)

    @pl.when(step == 0)
    def _():
        acc_ref[...] = jnp.zeros_like(acc_ref)

    acc_ref[...] += jnp.dot(conv_ref[0], w_ref[...], preferred_element_type=jnp.float32)

    @pl.when(step == pl.num_programs(0) - 1)
    def _():
        out_ref[...] = acc_ref[...].astype(jnp.bfloat16)


def scan_kernel(
    first_ref, conv_ref, proj_ref, dtw_ref, dtb_ref, alog_ref, skip_ref, out_ref,
    carry_ref, rate_ref, delta_ref, drive_ref, maps_ref, part_ref,
):
    step = pl.program_id(0)
    state, chans = alog_ref.shape
    rank = dtw_ref.shape[0]

    @pl.when(step == 0)
    def _():
        rate_ref[...] = jnp.exp(alog_ref[...]) * (-LOG2E)
        carry_ref[...] = jnp.zeros_like(carry_ref)

    @pl.when(first_ref[step] != 0)
    def _():
        carry_ref[...] = jnp.zeros_like(carry_ref)

    signal = conv_ref[...].astype(jnp.float32)
    summed = jnp.dot(proj_ref[:, :rank], dtw_ref[...], preferred_element_type=jnp.float32)
    delta = jax.nn.softplus(summed + dtb_ref[...].astype(jnp.float32))
    delta = delta.astype(jnp.bfloat16).astype(jnp.float32)
    delta_ref[...] = delta
    drive_ref[...] = delta * signal

    maps = proj_ref[:, rank:].astype(jnp.float32)
    pairs = maps.shape[1]
    spread = jnp.broadcast_to(maps[:, None, :], (BLK, state, pairs))
    place = lax.broadcasted_iota(jnp.int32, (BLK, state, pairs), 1)
    column = lax.broadcasted_iota(jnp.int32, (BLK, state, pairs), 2)
    keep = (column == place) | (column == place + state)
    spread = jnp.where(keep, spread, 0.0).reshape(BLK * state, pairs).astype(jnp.bfloat16)
    up = lax.broadcasted_iota(jnp.int32, (pairs, 2 * LANE), 0) < state
    left = lax.broadcasted_iota(jnp.int32, (pairs, 2 * LANE), 1) < LANE
    ones = jnp.where(up == left, 1.0, 0.0).astype(jnp.bfloat16)
    maps_ref[...] = jnp.dot(spread, ones, preferred_element_type=jnp.float32)

    halves = state // SUB
    tiles = chans // LANE
    rates = [
        [rate_ref[n * SUB : (n + 1) * SUB, c * LANE : (c + 1) * LANE] for c in range(tiles)]
        for n in range(halves)
    ]
    first = tuple(
        carry_ref[n * SUB : (n + 1) * SUB, c * LANE : (c + 1) * LANE]
        for n in range(halves)
        for c in range(tiles)
    )

    def advance(group, carry):
        carry = list(carry)
        rows = pl.ds(pl.multiple_of(group * SUB, SUB), SUB)
        deltas = delta_ref[rows, :]
        drives = drive_ref[rows, :]
        for inner in range(SUB):
            t = group * SUB + inner
            base = pl.multiple_of(t * state, state)
            in_map = [maps_ref[pl.ds(base + n * SUB, SUB), :LANE] for n in range(halves)]
            out_map = [maps_ref[pl.ds(base + n * SUB, SUB), LANE:] for n in range(halves)]
            for c in range(tiles):
                lanes = slice(c * LANE, (c + 1) * LANE)
                now = jnp.broadcast_to(deltas[inner : inner + 1, lanes], (SUB, LANE))
                drive = jnp.broadcast_to(drives[inner : inner + 1, lanes], (SUB, LANE))
                total = None
                for n in range(halves):
                    h = jnp.exp2(now * rates[n][c]) * carry[n * tiles + c] + drive * in_map[n]
                    carry[n * tiles + c] = h
                    total = h * out_map[n] if total is None else total + h * out_map[n]
                part_ref[c, pl.ds(pl.multiple_of(t * SUB, SUB), SUB), :] = total
        return tuple(carry)

    last = lax.fori_loop(0, BLK // SUB, advance, first)
    for n in range(halves):
        for c in range(tiles):
            carry_ref[n * SUB : (n + 1) * SUB, c * LANE : (c + 1) * LANE] = last[n * tiles + c]

    total = skip_ref[...] * conv_ref[...].astype(jnp.float32)
    for k in range(SUB):
        parts = [part_ref[c, pl.ds(k, BLK, stride=SUB), :] for c in range(tiles)]
        total = total + jnp.concatenate(parts, 1)
    out_ref[...] = total.astype(jnp.bfloat16)


def gate_kernel(live_ref, scanned_ref, gate_ref, out_ref):
    row = lax.broadcasted_iota(jnp.int32, (BLK, gate_ref.shape[1]), 0)
    for blk in range(gate_ref.shape[0] // BLK):
        rows = slice(blk * BLK, (blk + 1) * BLK)
        gated = scanned_ref[0, rows, :].astype(jnp.float32) * jax.nn.silu(
            gate_ref[rows, :].astype(jnp.float32)
        )
        out_ref[rows, :] = jnp.where(row < live_ref[blk], gated, 0.0).astype(jnp.bfloat16)


def body(
    mixer_in,
    gate_in,
    conv_weight,
    conv_bias,
    x_weight,
    dt_weight,
    dt_bias,
    a_log,
    d_skip,
    block_slot,
    block_first,
    block_live,
):
    ndev = lax.axis_size("dp")
    device = lax.axis_index("dp")
    tok_dev, width = mixer_in.shape
    taps = conv_weight.shape[0]
    state, chans = a_log.shape
    rank = dt_weight.shape[0]
    cols = x_weight.shape[1]
    per_dev = tok_dev // BLK
    total_tok = tok_dev * ndev
    local_first = lax.dynamic_slice_in_dim(block_first, device * per_dev, per_dev)
    local_live = lax.dynamic_slice_in_dim(block_live, device * per_dev, per_dev)
    x_all = lax.all_gather(x_weight, "dp", axis=0, tiled=True)
    halo = passed_along(mixer_in[tok_dev - HALO :], "dp", 1)
    smem = pl.BlockSpec(memory_space=pltpu.SMEM)

    convolved = pl.pallas_call(
        conv_kernel,
        grid=(ndev,),
        in_specs=[
            smem,
            pl.BlockSpec((tok_dev, chans), lambda i: (0, i)),
            pl.BlockSpec((HALO, chans), lambda i: (0, i)),
            pl.BlockSpec((taps, chans), lambda i: (0, i)),
            pl.BlockSpec((1, chans), lambda i: (0, i)),
        ],
        out_specs=pl.BlockSpec((1, tok_dev, chans), lambda i: (i, 0, 0)),
        out_shape=jax.ShapeDtypeStruct((ndev, tok_dev, chans), jnp.bfloat16),
        compiler_params=params(),
        cost_estimate=pl.CostEstimate(
            flops=20 * tok_dev * width, bytes_accessed=4 * tok_dev * width, transcendentals=0
        ),
        name="conv",
    )(local_first, mixer_in, halo, conv_weight, conv_bias[None])

    conv_chan = lax.all_to_all(convolved, "dp", split_axis=0, concat_axis=0, tiled=True)

    proj = pl.pallas_call(
        proj_kernel,
        grid=(ndev,),
        in_specs=[
            pl.BlockSpec((1, tok_dev, chans), lambda i: (i, 0, 0)),
            pl.BlockSpec((chans, cols), lambda i: (i, 0)),
        ],
        out_specs=pl.BlockSpec((tok_dev, cols), lambda i: (0, 0)),
        out_shape=jax.ShapeDtypeStruct((tok_dev, cols), jnp.bfloat16),
        scratch_shapes=[pltpu.VMEM((tok_dev, cols), jnp.float32)],
        compiler_params=params(),
        cost_estimate=pl.CostEstimate(
            flops=2 * tok_dev * width * cols,
            bytes_accessed=2 * (tok_dev + cols) * width,
            transcendentals=0,
        ),
        name="proj",
    )(convolved, x_all)
    proj_all = lax.all_gather(proj, "dp", axis=0, tiled=True)

    whole = lambda a, b: pl.BlockSpec((a, b), lambda i: (0, 0))
    scanned_chan = pl.pallas_call(
        scan_kernel,
        grid=(total_tok // BLK,),
        in_specs=[
            smem,
            pl.BlockSpec((BLK, chans), lambda i: (i, 0)),
            pl.BlockSpec((BLK, cols), lambda i: (i, 0)),
            whole(rank, chans),
            whole(1, chans),
            whole(state, chans),
            whole(1, chans),
        ],
        out_specs=pl.BlockSpec((BLK, chans), lambda i: (i, 0)),
        out_shape=jax.ShapeDtypeStruct((total_tok, chans), jnp.bfloat16),
        scratch_shapes=[
            pltpu.VMEM((state, chans), jnp.float32),
            pltpu.VMEM((state, chans), jnp.float32),
            pltpu.VMEM((BLK, chans), jnp.float32),
            pltpu.VMEM((BLK, chans), jnp.float32),
            pltpu.VMEM((BLK * state, 2 * LANE), jnp.float32),
            pltpu.VMEM((chans // LANE, BLK * SUB, LANE), jnp.float32),
        ],
        compiler_params=params(),
        name="scan",
    )(
        block_first,
        conv_chan.reshape(total_tok, chans),
        proj_all,
        dt_weight,
        dt_bias[None],
        a_log,
        d_skip[None],
    )

    scanned = lax.all_to_all(
        scanned_chan.reshape(ndev, tok_dev, chans), "dp", split_axis=0, concat_axis=0, tiled=True
    )
    return pl.pallas_call(
        gate_kernel,
        grid=(ndev,),
        in_specs=[
            smem,
            pl.BlockSpec((1, tok_dev, chans), lambda i: (i, 0, 0)),
            pl.BlockSpec((tok_dev, chans), lambda i: (0, i)),
        ],
        out_specs=pl.BlockSpec((tok_dev, chans), lambda i: (0, i)),
        out_shape=jax.ShapeDtypeStruct((tok_dev, width), jnp.bfloat16),
        compiler_params=params(),
        name="gate",
    )(local_live, scanned, gate_in)


def solution(mesh):
    in_specs = (
        P(("parts", "dp"), None),
        P(("parts", "dp"), None),
        P(),
        P(),
        P("dp", None),
        P(None, "dp"),
        P("dp"),
        P(None, "dp"),
        P("dp"),
        P("parts"),
        P("parts"),
        P("parts"),
    )
    out_specs = P(("parts", "dp"), None)
    return jax.shard_map(body, mesh=mesh, in_specs=in_specs, out_specs=out_specs, check_vma=False)
```

```python
import functools

import jax
import jax.numpy as jnp
from jax import lax
from jax.experimental import pallas as pl
from jax.experimental.pallas import tpu as pltpu
from jax.sharding import PartitionSpec as P

BLK = 128
SUB = 8
LANE = 128
HALO = 8
LOG2E = 1.4426950408889634
VMEM_LIMIT = 48 * 1024 * 1024


def passed_along(block, axis, distance):
    devices = range(lax.axis_size(axis))
    route = [(i - distance, i) for i in devices if i - distance in devices]
    return lax.ppermute(block, axis, route)


def params():
    return pltpu.CompilerParams(vmem_limit_bytes=VMEM_LIMIT)


def conv_kernel(first_ref, x_ref, halo_ref, w_ref, b_ref, out_ref):
    taps = w_ref.shape[0]
    w = w_ref[...].astype(jnp.float32)
    bias = b_ref[...].astype(jnp.float32)
    chans = x_ref.shape[1]
    row = lax.broadcasted_iota(jnp.int32, (SUB, chans), 0)
    before = halo_ref[...].astype(jnp.float32)
    for blk in range(x_ref.shape[0] // BLK):
        now = x_ref[blk * BLK : (blk + 1) * BLK, :].astype(jnp.float32)
        before = jnp.where(first_ref[blk] == 0, before, 0.0)
        acc = now * w[taps - 1 : taps] + bias
        for back in range(1, taps):
            rolled = pltpu.roll(now, back, 0)
            head = jnp.where(row < back, pltpu.roll(before, back, 0), rolled[:SUB])
            shifted = jnp.concatenate([head, rolled[SUB:]], 0)
            acc = acc + shifted * w[taps - 1 - back : taps - back]
        out_ref[0, blk * BLK : (blk + 1) * BLK, :] = jax.nn.silu(acc).astype(jnp.bfloat16)
        before = now[BLK - SUB :]


def proj_kernel(conv_ref, w_ref, out_ref):
    out_ref[0] = jnp.dot(conv_ref[0], w_ref[...], preferred_element_type=jnp.float32).astype(
        jnp.bfloat16
    )


def scan_kernel(
    first_ref, conv_ref, proj_ref, dtw_ref, dtb_ref, alog_ref, skip_ref, out_ref,
    carry_ref, rate_ref, delta_ref, drive_ref, maps_ref, part_ref,
):
    step = pl.program_id(0)
    state, chans = alog_ref.shape
    rank = dtw_ref.shape[0]

    @pl.when(step == 0)
    def _():
        rate_ref[...] = jnp.exp(alog_ref[...]) * (-LOG2E)
        carry_ref[...] = jnp.zeros_like(carry_ref)

    @pl.when(first_ref[step] != 0)
    def _():
        carry_ref[...] = jnp.zeros_like(carry_ref)

    signal = conv_ref[...].astype(jnp.float32)
    summed = jnp.dot(proj_ref[:, :rank], dtw_ref[...], preferred_element_type=jnp.float32)
    delta = jax.nn.softplus(summed + dtb_ref[...].astype(jnp.float32))
    delta = delta.astype(jnp.bfloat16).astype(jnp.float32)
    delta_ref[...] = delta
    drive_ref[...] = delta * signal

    maps = proj_ref[:, rank:].astype(jnp.float32)
    pairs = maps.shape[1]
    spread = jnp.broadcast_to(maps[:, None, :], (BLK, state, pairs))
    place = lax.broadcasted_iota(jnp.int32, (BLK, state, pairs), 1)
    column = lax.broadcasted_iota(jnp.int32, (BLK, state, pairs), 2)
    keep = (column == place) | (column == place + state)
    spread = jnp.where(keep, spread, 0.0).reshape(BLK * state, pairs).astype(jnp.bfloat16)
    up = lax.broadcasted_iota(jnp.int32, (pairs, 2 * LANE), 0) < state
    left = lax.broadcasted_iota(jnp.int32, (pairs, 2 * LANE), 1) < LANE
    ones = jnp.where(up == left, 1.0, 0.0).astype(jnp.bfloat16)
    maps_ref[...] = jnp.dot(spread, ones, preferred_element_type=jnp.float32)

    halves = state // SUB
    tiles = chans // LANE
    rates = [
        [rate_ref[n * SUB : (n + 1) * SUB, c * LANE : (c + 1) * LANE] for c in range(tiles)]
        for n in range(halves)
    ]
    first = tuple(
        carry_ref[n * SUB : (n + 1) * SUB, c * LANE : (c + 1) * LANE]
        for n in range(halves)
        for c in range(tiles)
    )

    def advance(group, carry):
        carry = list(carry)
        rows = pl.ds(pl.multiple_of(group * SUB, SUB), SUB)
        deltas = delta_ref[rows, :]
        drives = drive_ref[rows, :]
        for inner in range(SUB):
            t = group * SUB + inner
            base = pl.multiple_of(t * state, state)
            in_map = [maps_ref[pl.ds(base + n * SUB, SUB), :LANE] for n in range(halves)]
            out_map = [maps_ref[pl.ds(base + n * SUB, SUB), LANE:] for n in range(halves)]
            for c in range(tiles):
                lanes = slice(c * LANE, (c + 1) * LANE)
                now = jnp.broadcast_to(deltas[inner : inner + 1, lanes], (SUB, LANE))
                drive = jnp.broadcast_to(drives[inner : inner + 1, lanes], (SUB, LANE))
                total = None
                for n in range(halves):
                    h = jnp.exp2(now * rates[n][c]) * carry[n * tiles + c] + drive * in_map[n]
                    carry[n * tiles + c] = h
                    total = h * out_map[n] if total is None else total + h * out_map[n]
                part_ref[c, pl.ds(pl.multiple_of(t * SUB, SUB), SUB), :] = total
        return tuple(carry)

    last = lax.fori_loop(0, BLK // SUB, advance, first)
    for n in range(halves):
        for c in range(tiles):
            carry_ref[n * SUB : (n + 1) * SUB, c * LANE : (c + 1) * LANE] = last[n * tiles + c]

    total = skip_ref[...] * conv_ref[...].astype(jnp.float32)
    for k in range(SUB):
        parts = [part_ref[c, pl.ds(k, BLK, stride=SUB), :] for c in range(tiles)]
        total = total + jnp.concatenate(parts, 1)
    out_ref[...] = total.astype(jnp.bfloat16)


def gate_kernel(pieces, live_ref, *refs):
    gate_ref, out_ref = refs[pieces:]
    chans = refs[0].shape[2]
    row = lax.broadcasted_iota(jnp.int32, (BLK, chans), 0)
    for blk in range(gate_ref.shape[0] // BLK):
        rows = slice(blk * BLK, (blk + 1) * BLK)
        for piece in range(pieces):
            lanes = slice(piece * chans, (piece + 1) * chans)
            gated = refs[piece][0, rows, :].astype(jnp.float32) * jax.nn.silu(
                gate_ref[rows, lanes].astype(jnp.float32)
            )
            gated = jnp.where(row < live_ref[blk], gated, 0.0)
            out_ref[rows, lanes] = gated.astype(jnp.bfloat16)


def body(
    mixer_in,
    gate_in,
    conv_weight,
    conv_bias,
    x_weight,
    dt_weight,
    dt_bias,
    a_log,
    d_skip,
    block_slot,
    block_first,
    block_live,
):
    ndev = lax.axis_size("dp")
    device = lax.axis_index("dp")
    tok_dev, width = mixer_in.shape
    taps = conv_weight.shape[0]
    state, chans = a_log.shape
    rank = dt_weight.shape[0]
    cols = x_weight.shape[1]
    per_dev = tok_dev // BLK
    total_tok = tok_dev * ndev
    local_first = lax.dynamic_slice_in_dim(block_first, device * per_dev, per_dev)
    local_live = lax.dynamic_slice_in_dim(block_live, device * per_dev, per_dev)
    halo = passed_along(mixer_in[tok_dev - HALO :], "dp", 1)
    smem = pl.BlockSpec(memory_space=pltpu.SMEM)

    convolved = pl.pallas_call(
        conv_kernel,
        grid=(ndev,),
        in_specs=[
            smem,
            pl.BlockSpec((tok_dev, chans), lambda i: (0, i)),
            pl.BlockSpec((HALO, chans), lambda i: (0, i)),
            pl.BlockSpec((taps, chans), lambda i: (0, i)),
            pl.BlockSpec((1, chans), lambda i: (0, i)),
        ],
        out_specs=pl.BlockSpec((1, tok_dev, chans), lambda i: (i, 0, 0)),
        out_shape=jax.ShapeDtypeStruct((ndev, tok_dev, chans), jnp.bfloat16),
        compiler_params=params(),
        cost_estimate=pl.CostEstimate(
            flops=20 * tok_dev * width, bytes_accessed=4 * tok_dev * width, transcendentals=0
        ),
        name="conv",
    )(local_first, mixer_in, halo, conv_weight, conv_bias[None])

    conv_chan = lax.all_to_all(convolved, "dp", split_axis=0, concat_axis=0, tiled=True)

    shares = pl.pallas_call(
        proj_kernel,
        grid=(ndev,),
        in_specs=[
            pl.BlockSpec((1, tok_dev, chans), lambda i: (i, 0, 0)),
            pl.BlockSpec((chans, cols), lambda i: (0, 0)),
        ],
        out_specs=pl.BlockSpec((1, tok_dev, cols), lambda i: (i, 0, 0)),
        out_shape=jax.ShapeDtypeStruct((ndev, tok_dev, cols), jnp.bfloat16),
        compiler_params=params(),
        name="proj",
    )(conv_chan, x_weight)
    shares = lax.all_to_all(shares, "dp", split_axis=0, concat_axis=0, tiled=True)
    proj = jnp.sum(shares.astype(jnp.float32), axis=0).astype(jnp.bfloat16)
    proj_all = lax.all_to_all(
        jnp.broadcast_to(proj[None], (ndev, tok_dev, cols)),
        "dp",
        split_axis=0,
        concat_axis=0,
        tiled=True,
    ).reshape(total_tok, cols)

    pieces = 2 if chans % (2 * LANE) == 0 else 1
    chans = chans // pieces
    scanned = []
    for piece in range(pieces):
        part = lambda a, k=piece: pl.BlockSpec((a, chans), lambda i: (0, k))
        scanned_chan = pl.pallas_call(
            scan_kernel,
            grid=(total_tok // BLK,),
            in_specs=[
                smem,
                pl.BlockSpec((BLK, chans), lambda i, k=piece: (i, k)),
                pl.BlockSpec((BLK, cols), lambda i: (i, 0)),
                part(rank),
                part(1),
                part(state),
                part(1),
            ],
            out_specs=pl.BlockSpec((BLK, chans), lambda i: (i, 0)),
            out_shape=jax.ShapeDtypeStruct((total_tok, chans), jnp.bfloat16),
            scratch_shapes=[
                pltpu.VMEM((state, chans), jnp.float32),
                pltpu.VMEM((state, chans), jnp.float32),
                pltpu.VMEM((BLK, chans), jnp.float32),
                pltpu.VMEM((BLK, chans), jnp.float32),
                pltpu.VMEM((BLK * state, 2 * LANE), jnp.float32),
                pltpu.VMEM((chans // LANE, BLK * SUB, LANE), jnp.float32),
            ],
            compiler_params=params(),
            name="scan",
        )(
            block_first,
            conv_chan.reshape(total_tok, pieces * chans),
            proj_all,
            dt_weight,
            dt_bias[None],
            a_log,
            d_skip[None],
        )

        scanned.append(
            lax.all_to_all(
                scanned_chan.reshape(ndev, tok_dev, chans),
                "dp",
                split_axis=0,
                concat_axis=0,
                tiled=True,
            )
        )
    return pl.pallas_call(
        functools.partial(gate_kernel, pieces),
        grid=(ndev,),
        in_specs=[smem]
        + [pl.BlockSpec((1, tok_dev, chans), lambda i: (i, 0, 0))] * pieces
        + [pl.BlockSpec((tok_dev, pieces * chans), lambda i: (0, i))],
        out_specs=pl.BlockSpec((tok_dev, pieces * chans), lambda i: (0, i)),
        out_shape=jax.ShapeDtypeStruct((tok_dev, width), jnp.bfloat16),
        compiler_params=params(),
        name="gate",
    )(local_live, *scanned, gate_in)


def solution(mesh):
    in_specs = (
        P(("parts", "dp"), None),
        P(("parts", "dp"), None),
        P(),
        P(),
        P("dp", None),
        P(None, "dp"),
        P("dp"),
        P(None, "dp"),
        P("dp"),
        P("parts"),
        P("parts"),
        P("parts"),
    )
    out_specs = P(("parts", "dp"), None)
    return jax.shard_map(body, mesh=mesh, in_specs=in_specs, out_specs=out_specs, check_vma=False)
```

```python
import jax
import jax.numpy as jnp
from jax import lax
from jax.experimental import pallas as pl
from jax.experimental.pallas import tpu as pltpu
from jax.sharding import PartitionSpec as P

BLK = 128
SUB = 8
LANE = 128
HALO = 8
LOG2E = 1.4426950408889634
VMEM_LIMIT = 48 * 1024 * 1024


def passed_along(block, axis, distance):
    devices = range(lax.axis_size(axis))
    route = [(i - distance, i) for i in devices if i - distance in devices]
    return lax.ppermute(block, axis, route)


def params():
    return pltpu.CompilerParams(vmem_limit_bytes=VMEM_LIMIT)


def conv_kernel(first_ref, x_ref, halo_ref, w_ref, b_ref, out_ref):
    taps = w_ref.shape[0]
    w = w_ref[...].astype(jnp.float32)
    bias = b_ref[...].astype(jnp.float32)
    chans = x_ref.shape[1]
    row = lax.broadcasted_iota(jnp.int32, (SUB, chans), 0)
    before = halo_ref[...].astype(jnp.float32)
    for blk in range(x_ref.shape[0] // BLK):
        now = x_ref[blk * BLK : (blk + 1) * BLK, :].astype(jnp.float32)
        before = jnp.where(first_ref[blk] == 0, before, 0.0)
        acc = now * w[taps - 1 : taps] + bias
        for back in range(1, taps):
            rolled = pltpu.roll(now, back, 0)
            head = jnp.where(row < back, pltpu.roll(before, back, 0), rolled[:SUB])
            shifted = jnp.concatenate([head, rolled[SUB:]], 0)
            acc = acc + shifted * w[taps - 1 - back : taps - back]
        out_ref[0, blk * BLK : (blk + 1) * BLK, :] = jax.nn.silu(acc).astype(jnp.bfloat16)
        before = now[BLK - SUB :]


def proj_kernel(conv_ref, rank_ref, maps_ref, out_ref, acc_ref):
    step = pl.program_id(0)
    rank = rank_ref.shape[1]

    @pl.when(step == 0)
    def _():
        acc_ref[...] = jnp.zeros_like(acc_ref)

    acc_ref[:, :rank] += jnp.dot(conv_ref[0], rank_ref[...], preferred_element_type=jnp.float32)
    acc_ref[:, rank:] += lax.dot_general(
        conv_ref[0], maps_ref[0], (((1,), (1,)), ((), ())), preferred_element_type=jnp.float32
    )

    @pl.when(step == pl.num_programs(0) - 1)
    def _():
        out_ref[...] = acc_ref[...].astype(jnp.bfloat16)


def scan_kernel(
    first_ref, conv_ref, proj_ref, dtw_ref, dtb_ref, alog_ref, skip_ref, out_ref,
    carry_ref, rate_ref, delta_ref, drive_ref, maps_ref, part_ref,
):
    step = pl.program_id(0)
    state, chans = alog_ref.shape
    rank = dtw_ref.shape[0]

    @pl.when(step == 0)
    def _():
        rate_ref[...] = jnp.exp(alog_ref[...]) * (-LOG2E)
        carry_ref[...] = jnp.zeros_like(carry_ref)

    @pl.when(first_ref[step] != 0)
    def _():
        carry_ref[...] = jnp.zeros_like(carry_ref)

    signal = conv_ref[...].astype(jnp.float32)
    summed = jnp.dot(proj_ref[:, :rank], dtw_ref[...], preferred_element_type=jnp.float32)
    delta = jax.nn.softplus(summed + dtb_ref[...].astype(jnp.float32))
    delta = delta.astype(jnp.bfloat16).astype(jnp.float32)
    delta_ref[...] = delta
    drive_ref[...] = delta * signal

    maps = proj_ref[:, rank:].astype(jnp.float32)
    pairs = maps.shape[1]
    spread = jnp.broadcast_to(maps[:, None, :], (BLK, state, pairs))
    place = lax.broadcasted_iota(jnp.int32, (BLK, state, pairs), 1)
    column = lax.broadcasted_iota(jnp.int32, (BLK, state, pairs), 2)
    keep = (column == place) | (column == place + state)
    spread = jnp.where(keep, spread, 0.0).reshape(BLK * state, pairs).astype(jnp.bfloat16)
    up = lax.broadcasted_iota(jnp.int32, (pairs, 2 * LANE), 0) < state
    left = lax.broadcasted_iota(jnp.int32, (pairs, 2 * LANE), 1) < LANE
    ones = jnp.where(up == left, 1.0, 0.0).astype(jnp.bfloat16)
    maps_ref[...] = jnp.dot(spread, ones, preferred_element_type=jnp.float32)

    halves = state // SUB
    tiles = chans // LANE
    rates = [
        [rate_ref[n * SUB : (n + 1) * SUB, c * LANE : (c + 1) * LANE] for c in range(tiles)]
        for n in range(halves)
    ]
    first = tuple(
        carry_ref[n * SUB : (n + 1) * SUB, c * LANE : (c + 1) * LANE]
        for n in range(halves)
        for c in range(tiles)
    )

    def advance(group, carry):
        carry = list(carry)
        rows = pl.ds(pl.multiple_of(group * SUB, SUB), SUB)
        deltas = delta_ref[rows, :]
        drives = drive_ref[rows, :]
        for inner in range(SUB):
            t = group * SUB + inner
            base = pl.multiple_of(t * state, state)
            in_map = [maps_ref[pl.ds(base + n * SUB, SUB), :LANE] for n in range(halves)]
            out_map = [maps_ref[pl.ds(base + n * SUB, SUB), LANE:] for n in range(halves)]
            for c in range(tiles):
                lanes = slice(c * LANE, (c + 1) * LANE)
                now = jnp.broadcast_to(deltas[inner : inner + 1, lanes], (SUB, LANE))
                drive = jnp.broadcast_to(drives[inner : inner + 1, lanes], (SUB, LANE))
                total = None
                for n in range(halves):
                    h = jnp.exp2(now * rates[n][c]) * carry[n * tiles + c] + drive * in_map[n]
                    carry[n * tiles + c] = h
                    total = h * out_map[n] if total is None else total + h * out_map[n]
                part_ref[c, pl.ds(pl.multiple_of(t * SUB, SUB), SUB), :] = total
        return tuple(carry)

    last = lax.fori_loop(0, BLK // SUB, advance, first)
    for n in range(halves):
        for c in range(tiles):
            carry_ref[n * SUB : (n + 1) * SUB, c * LANE : (c + 1) * LANE] = last[n * tiles + c]

    total = skip_ref[...] * conv_ref[...].astype(jnp.float32)
    for k in range(SUB):
        parts = [part_ref[c, pl.ds(k, BLK, stride=SUB), :] for c in range(tiles)]
        total = total + jnp.concatenate(parts, 1)
    out_ref[...] = total.astype(jnp.bfloat16)


def gate_kernel(live_ref, scanned_ref, gate_ref, out_ref):
    row = lax.broadcasted_iota(jnp.int32, (BLK, gate_ref.shape[1]), 0)
    for blk in range(gate_ref.shape[0] // BLK):
        rows = slice(blk * BLK, (blk + 1) * BLK)
        gated = scanned_ref[0, rows, :].astype(jnp.float32) * jax.nn.silu(
            gate_ref[rows, :].astype(jnp.float32)
        )
        out_ref[rows, :] = jnp.where(row < live_ref[blk], gated, 0.0).astype(jnp.bfloat16)


def body(
    mixer_in,
    gate_in,
    conv_weight,
    conv_bias,
    x_weight,
    dt_weight,
    dt_bias,
    a_log,
    d_skip,
    block_slot,
    block_first,
    block_live,
):
    ndev = lax.axis_size("dp")
    device = lax.axis_index("dp")
    tok_dev, width = mixer_in.shape
    taps = conv_weight.shape[0]
    state, chans = a_log.shape
    rank = dt_weight.shape[0]
    cols = x_weight.shape[1]
    per_dev = tok_dev // BLK
    total_tok = tok_dev * ndev
    local_first = lax.dynamic_slice_in_dim(block_first, device * per_dev, per_dev)
    local_live = lax.dynamic_slice_in_dim(block_live, device * per_dev, per_dev)
    rank_all = lax.all_gather(x_weight[:, :rank], "dp", axis=0, tiled=True)
    maps_all = lax.all_gather(x_weight[:, rank:].T, "dp", axis=0, tiled=False)
    halo = passed_along(mixer_in[tok_dev - HALO :], "dp", 1)
    smem = pl.BlockSpec(memory_space=pltpu.SMEM)

    convolved = pl.pallas_call(
        conv_kernel,
        grid=(ndev,),
        in_specs=[
            smem,
            pl.BlockSpec((tok_dev, chans), lambda i: (0, i)),
            pl.BlockSpec((HALO, chans), lambda i: (0, i)),
            pl.BlockSpec((taps, chans), lambda i: (0, i)),
            pl.BlockSpec((1, chans), lambda i: (0, i)),
        ],
        out_specs=pl.BlockSpec((1, tok_dev, chans), lambda i: (i, 0, 0)),
        out_shape=jax.ShapeDtypeStruct((ndev, tok_dev, chans), jnp.bfloat16),
        compiler_params=params(),
        cost_estimate=pl.CostEstimate(
            flops=20 * tok_dev * width, bytes_accessed=4 * tok_dev * width, transcendentals=0
        ),
        name="conv",
    )(local_first, mixer_in, halo, conv_weight, conv_bias[None])

    conv_chan = lax.all_to_all(convolved, "dp", split_axis=0, concat_axis=0, tiled=True)

    proj = pl.pallas_call(
        proj_kernel,
        grid=(ndev,),
        in_specs=[
            pl.BlockSpec((1, tok_dev, chans), lambda i: (i, 0, 0)),
            pl.BlockSpec((chans, rank), lambda i: (i, 0)),
            pl.BlockSpec((1, cols - rank, chans), lambda i: (i, 0, 0)),
        ],
        out_specs=pl.BlockSpec((tok_dev, cols), lambda i: (0, 0)),
        out_shape=jax.ShapeDtypeStruct((tok_dev, cols), jnp.bfloat16),
        scratch_shapes=[pltpu.VMEM((tok_dev, cols), jnp.float32)],
        compiler_params=params(),
        cost_estimate=pl.CostEstimate(
            flops=2 * tok_dev * width * cols,
            bytes_accessed=2 * (tok_dev + cols) * width,
            transcendentals=0,
        ),
        name="proj",
    )(convolved, rank_all, maps_all)
    proj_all = lax.all_gather(proj, "dp", axis=0, tiled=True)

    whole = lambda a, b: pl.BlockSpec((a, b), lambda i: (0, 0))
    scanned_chan = pl.pallas_call(
        scan_kernel,
        grid=(total_tok // BLK,),
        in_specs=[
            smem,
            pl.BlockSpec((BLK, chans), lambda i: (i, 0)),
            pl.BlockSpec((BLK, cols), lambda i: (i, 0)),
            whole(rank, chans),
            whole(1, chans),
            whole(state, chans),
            whole(1, chans),
        ],
        out_specs=pl.BlockSpec((BLK, chans), lambda i: (i, 0)),
        out_shape=jax.ShapeDtypeStruct((total_tok, chans), jnp.bfloat16),
        scratch_shapes=[
            pltpu.VMEM((state, chans), jnp.float32),
            pltpu.VMEM((state, chans), jnp.float32),
            pltpu.VMEM((BLK, chans), jnp.float32),
            pltpu.VMEM((BLK, chans), jnp.float32),
            pltpu.VMEM((BLK * state, 2 * LANE), jnp.float32),
            pltpu.VMEM((chans // LANE, BLK * SUB, LANE), jnp.float32),
        ],
        compiler_params=params(),
        name="scan",
    )(
        block_first,
        conv_chan.reshape(total_tok, chans),
        proj_all,
        dt_weight,
        dt_bias[None],
        a_log,
        d_skip[None],
    )

    scanned = lax.all_to_all(
        scanned_chan.reshape(ndev, tok_dev, chans), "dp", split_axis=0, concat_axis=0, tiled=True
    )
    return pl.pallas_call(
        gate_kernel,
        grid=(ndev,),
        in_specs=[
            smem,
            pl.BlockSpec((1, tok_dev, chans), lambda i: (i, 0, 0)),
            pl.BlockSpec((tok_dev, chans), lambda i: (0, i)),
        ],
        out_specs=pl.BlockSpec((tok_dev, chans), lambda i: (0, i)),
        out_shape=jax.ShapeDtypeStruct((tok_dev, width), jnp.bfloat16),
        compiler_params=params(),
        name="gate",
    )(local_live, scanned, gate_in)


def solution(mesh):
    in_specs = (
        P(("parts", "dp"), None),
        P(("parts", "dp"), None),
        P(),
        P(),
        P("dp", None),
        P(None, "dp"),
        P("dp"),
        P(None, "dp"),
        P("dp"),
        P("parts"),
        P("parts"),
        P("parts"),
    )
    out_specs = P(("parts", "dp"), None)
    return jax.shard_map(body, mesh=mesh, in_specs=in_specs, out_specs=out_specs, check_vma=False)
```
